512 devices in a mesh: dp: 128 (over z_lo, x, y), slab: 4 (over z_hi, core).
Axes of the slice: x: 4, y: 8, z: 8 (z_hi: 2, z_lo: 4; z = z_hi * 4 + z_lo), core: 2. Of those that a mesh axis runs over, the one named last changes fastest.
Arguments:
- features: bfloat16 [128, 48, 40, 2048], P('dp', 'slab'), may hold values from -6 to 6
- labels: int32 [128, 48, 40], P('dp', 'slab'), may hold values from 0 to 2
- cotangent: bfloat16 [128, 48, 40, 256], P('dp', 'slab'), may hold values from -6 to 6
- first_kernel: float32 [3, 3, 2048], replicated, may hold values from -2 to 2
- holed_kernel: float32 [3, 3, 2048], replicated, may hold values from -2 to 2
- point_weight: bfloat16 [2048, 256], replicated, may hold values from -0.125 to 0.125
Outputs:
- branch_out: bfloat16 [128, 48, 40, 256], P('dp', 'slab')
- point_grad: bfloat16 [2048, 256], replicated
- first_grad: float32 [3, 3, 2048], replicated
- atrous_grad: float32 [3, 3, 2048], replicated
The draws below stay inside these ranges and needn't reach their ends.
All inputs are finite; a program needn't handle non-finite values.
Results may differ from the reference program's by a relative error of at most 0.015.
Values may be sent and summed in bfloat16 or wider, within the bound.
No kernel may reach another device: no remote copies, remote signals or barrier semaphores. Data moves between devices by JAX's collectives and lax.ppermute only.
A program may use at most 128 MiB of HBM per device.

```python
import math
import jax
import jax.numpy as jnp
from jax import lax

C = 2048
F = 256
DILATION_STEP = 36
LONGITUDE_COLUMNS = 40
SAMPLES = 128
LATITUDE_ROWS = 48


def plant(values, key, smallest, top_value):
    spot = [jax.random.randint(jax.random.fold_in(key, axis), (), 0, length) for axis, length in enumerate(values.shape)]
    main_axis = values.shape.index(max(values.shape))
    beside = spot[:main_axis] + [(spot[main_axis] + 1) % values.shape[main_axis]] + spot[main_axis + 1:]
    return values.at[tuple(spot)].set(smallest).at[tuple(beside)].set(top_value)


def shard_levels(stream_key, dims, cuts, least, largest):
    gain = 1.0
    for axis_at, blocks in cuts:
        draws = jax.random.uniform(jax.random.fold_in(jax.random.fold_in(stream_key, 6), axis_at), (blocks,), jnp.float32, least / len(cuts), largest / len(cuts))
        gain = gain * jnp.repeat(jnp.exp(draws), dims[axis_at] // blocks).reshape((-1,) + (1,) * (len(dims) - 1 - axis_at))
    return gain


def scatter_about(key, dims, scale, reach, shards=(), dtype=jnp.bfloat16):
    level = shard_levels(key, dims, shards, -0.22, 0.18) if shards else 1.0
    values = jax.random.normal(key, dims, jnp.float32) * scale * level
    return jnp.minimum(jnp.maximum(values, -reach), reach).astype(dtype)


def setup_inputs(seed: int = 0) -> dict:
    arg_keys = jax.random.split(jax.random.key(seed), 7)
    return {
        "features": scatter_about(arg_keys[0], (SAMPLES, LATITUDE_ROWS, LONGITUDE_COLUMNS, C), 1.0, 6.0, ((0, 128), (1, 4))),
        "labels": plant(jax.random.randint(arg_keys[1], (SAMPLES, LATITUDE_ROWS, LONGITUDE_COLUMNS), 0, 3), jax.random.fold_in(arg_keys[1], 1), 0, 2).astype(jnp.int32),
        "cotangent": scatter_about(arg_keys[2], (SAMPLES, LATITUDE_ROWS, LONGITUDE_COLUMNS, F), 1.0, 6.0, ((0, 128), (1, 4))),
        "first_kernel": scatter_about(arg_keys[3], (3, 3, C), 0.35, 2.0, (), jnp.float32),
        "holed_kernel": scatter_about(arg_keys[4], (3, 3, C), 0.35, 2.0, (), jnp.float32),
        "point_weight": scatter_about(arg_keys[5], (C, F), C ** -0.5, 0.125),
    }


def class_weighting(labels):
    return jnp.where(labels == 0, 0.6, jnp.where(labels == 1, 2.4, 1.5)).astype(jnp.float32)

def kernel_tap_window(padded, kernel, row_count, column_count, stride):
    summed = jnp.zeros((row_count, column_count, padded.shape[2]), jnp.float32)
    for row_tap in range(3):
        for col_tap in range(3):
            window = padded[row_tap * stride:row_tap * stride + row_count, col_tap * stride:col_tap * stride + column_count]
            summed = summed + kernel[row_tap, col_tap] * window
    return summed

def kernel_tap_product(padded, gradient, row_count, column_count, stride):
    pieces = []
    for row_tap in range(3):
        for col_tap in range(3):
            window = padded[row_tap * stride:row_tap * stride + row_count, col_tap * stride:col_tap * stride + column_count]
            pieces.append(lax.optimization_barrier(jnp.sum(window * gradient, axis=(0, 1))))
    return jnp.stack(pieces).reshape(3, 3, -1)

def reference(features, labels, cotangent, first_kernel, holed_kernel, point_weight):

    def one_sample(running_total, sample):
        feat_one, label_one, cot_one = sample
        padded_in = jnp.pad(feat_one.astype(jnp.float32), ((1, 1), (1, 1), (0, 0)))
        first = kernel_tap_window(padded_in, first_kernel, LATITUDE_ROWS, LONGITUDE_COLUMNS, 1).astype(jnp.bfloat16)
        leading_widened = lax.optimization_barrier(first).astype(jnp.float32)
        leading_padded = jnp.pad(leading_widened, ((DILATION_STEP, DILATION_STEP), (DILATION_STEP, DILATION_STEP), (0, 0)))
        holed_output = kernel_tap_window(leading_padded, holed_kernel, LATITUDE_ROWS, LONGITUDE_COLUMNS, DILATION_STEP).astype(jnp.bfloat16)
        atrous_flat = holed_output.reshape(LATITUDE_ROWS * LONGITUDE_COLUMNS, C)
        out_one = jnp.dot(atrous_flat, point_weight, preferred_element_type=jnp.float32).astype(jnp.bfloat16)
        weighted = (cot_one.astype(jnp.float32) * class_weighting(label_one)[:, :, None]).astype(jnp.bfloat16)
        weighted_flat = weighted.reshape(LATITUDE_ROWS * LONGITUDE_COLUMNS, F)
        holed_gradient = jnp.dot(weighted_flat, point_weight.T, preferred_element_type=jnp.float32).astype(jnp.bfloat16)
        point_sum = running_total[0] + jnp.dot(atrous_flat.T, weighted_flat, preferred_element_type=jnp.float32)
        gradient_widened = lax.optimization_barrier(holed_gradient).astype(jnp.float32).reshape(LATITUDE_ROWS, LONGITUDE_COLUMNS, C)
        holed_total_sum = running_total[1] + kernel_tap_product(leading_padded, gradient_widened, LATITUDE_ROWS, LONGITUDE_COLUMNS, DILATION_STEP)
        gradient_padded = jnp.pad(gradient_widened, ((DILATION_STEP, DILATION_STEP), (DILATION_STEP, DILATION_STEP), (0, 0)))
        leading_gradient = kernel_tap_window(gradient_padded, holed_kernel[::-1, ::-1], LATITUDE_ROWS, LONGITUDE_COLUMNS, DILATION_STEP).astype(jnp.bfloat16)
        first_back_wide = lax.optimization_barrier(leading_gradient).astype(jnp.float32)
        first_sum = running_total[2] + kernel_tap_product(padded_in, first_back_wide, LATITUDE_ROWS, LONGITUDE_COLUMNS, 1)
        return ((point_sum, holed_total_sum, first_sum), out_one.reshape(LATITUDE_ROWS, LONGITUDE_COLUMNS, F))
    start = (jnp.zeros((C, F), jnp.float32), jnp.zeros((3, 3, C), jnp.float32), jnp.zeros((3, 3, C), jnp.float32))
    sums, branch_out = lax.scan(one_sample, start, (features, labels, cotangent))
    scale = 1.0 / math.sqrt(SAMPLES * LATITUDE_ROWS * LONGITUDE_COLUMNS)
    point_grad = (sums[0] * scale).astype(jnp.bfloat16)
    return (branch_out, point_grad, sums[2] * scale, sums[1] * scale)
```

```python
import itertools
import math

import jax
import jax.numpy as jnp
from jax import lax
from jax.experimental import pallas as pl
from jax.experimental.pallas import tpu as pltpu
from jax.sharding import PartitionSpec as P

AXES = ("dp", "slab")
STEP = 36
ROWS = 12
COLS = 40
CELLS = ROWS * COLS
EDGE = COLS - STEP
CHANNELS = 2048
WIDTH = 256
BLOCK = 256
LANES = 128
GRAD_ROWS = 32
PAYLOAD_ROWS = 2 * CHANNELS + CHANNELS // LANES * GRAD_ROWS
F32 = jnp.float32
BF16 = jnp.bfloat16


def device_groups(dims, *names):
    strides, stride = {}, 1
    for name in reversed(dims):
        strides[name] = stride
        stride *= dims[name]

    def places(chosen):
        return [
            sum(i * strides[n] for n, i in zip(chosen, spot))
            for spot in itertools.product(*(range(dims[n]) for n in chosen))
        ]

    inside = places(names)
    return [[base + i for i in inside] for base in places([n for n in dims if n not in names])]


def exchange(parts, groups):
    return lax.all_to_all(parts, AXES, 0, 0, axis_index_groups=groups, tiled=True)


def scattered(units, groups):
    count = len(groups[0])
    parts = exchange(units.reshape(count, units.shape[0] // count, 8, LANES), groups)
    return jnp.sum(parts.astype(F32), axis=0)


def gathered(units, groups):
    count = len(groups[0])
    return exchange(jnp.broadcast_to(units[None], (count, *units.shape)), groups)


def body(
    slab_ref,
    x_ref,
    near_ref,
    far_ref,
    weighted_ref,
    partner_ref,
    first_k_ref,
    holed_k_ref,
    point_ref,
    payload_ref,
    own_out_ref,
    far_out_ref,
    xs,
    wfar,
    b_own,
    b_far,
    a_own,
    a_far,
    own_acc,
    far_acc,
):
    step = pl.program_id(0)
    slab = slab_ref[0]
    core = lax.rem(slab, 2)
    outer = jnp.logical_or(slab == 0, slab == 3)

    @pl.when(step == 0)
    def _():
        keep = jnp.where(outer, 1.0, 0.0)
        wfar[...] = (partner_ref[...].astype(F32) * keep).astype(BF16)
        own_acc[...] = jnp.zeros_like(own_acc)
        far_acc[...] = jnp.zeros_like(far_acc)

    near = near_ref[...].astype(F32)
    far = far_ref[...].astype(F32)
    is_one = jnp.where(core == 1, 1.0, 0.0)
    is_zero = 1.0 - is_one
    xs[pl.ds(0, COLS), :] = near * is_one + far * jnp.where(slab == 2, 1.0, 0.0)
    xs[pl.ds((ROWS + 1) * COLS, COLS), :] = near * is_zero + far * jnp.where(slab == 1, 1.0, 0.0)

    def widen(r, _):
        xs[pl.ds(pl.multiple_of((r + 1) * COLS, 8), COLS), :] = x_ref[r].astype(F32)
        return 0

    lax.fori_loop(0, ROWS, widen, 0)

    weights = point_ref[...]
    nt = (((1,), (1,)), ((), ()))
    tn = (((0,), (0,)), ((), ()))
    b_own[...] = (
        lax.dot_general(weighted_ref[...], weights, nt, preferred_element_type=F32)
        .astype(BF16)
        .astype(F32)
    )
    b_far[...] = (
        lax.dot_general(wfar[...], weights, nt, preferred_element_type=F32)
        .astype(BF16)
        .astype(F32)
    )

    col = lax.broadcasted_iota(jnp.int32, (COLS, LANES), 0)
    sub = lax.broadcasted_iota(jnp.int32, (8, LANES), 0)
    low = sub < EDGE
    up_f = jnp.where(slab == 0, 1.0, 0.0)
    down_f = jnp.where(slab == 3, 1.0, 0.0)

    def from_left(v):
        return jnp.where(col == 0, 0.0, pltpu.roll(v, 1, 0))

    def from_right(v):
        return jnp.where(col == COLS - 1, 0.0, pltpu.roll(v, COLS - 1, 0))

    def fold(v):
        parts = [v[8 * i : 8 * i + 8] for i in range(COLS // 8)]
        while len(parts) > 1:
            parts = [a + b for a, b in zip(parts[::2], parts[1::2])] + (
                parts[-1:] if len(parts) % 2 else []
            )
        return parts[0]

    for chunk in range(BLOCK // LANES):
        lanes = pl.ds(chunk * LANES, LANES)
        fk = [[first_k_ref[i, j : j + 1, lanes] for j in range(3)] for i in range(3)]
        hk = [[holed_k_ref[i, j : j + 1, lanes] for j in range(3)] for i in range(3)]
        mk = hk[1]
        kf = [hk[0][j] * up_f + hk[2][j] * down_f for j in range(3)]

        def pair(p, acc, lanes=lanes, fk=fk, mk=mk, kf=kf):
            first_acc, own_g, far_g = [list(a) for a in acc]
            base = pl.multiple_of(p * 2 * COLS, 2 * COLS)
            x = [xs[pl.ds(pl.multiple_of(base + i * COLS, 8), COLS), lanes] for i in range(4)]
            own_rows, far_rows = [], []
            for r in range(2):
                side = [
                    fk[0][j] * x[r] + fk[1][j] * x[r + 1] + fk[2][j] * x[r + 2] for j in range(3)
                ]
                f = side[1] + from_left(side[0]) + from_right(side[2])
                f = f.astype(BF16).astype(F32)
                here = pl.ds(pl.multiple_of(base + r * COLS, 8), COLS)
                bo, bf = b_own[here, lanes], b_far[here, lanes]
                f_hi = jnp.where(low, pltpu.roll(f[STEP - EDGE :], 4, 0), 0.0)
                f_lo = jnp.where(low, 0.0, pltpu.roll(f[:8], 4, 0))

                def spread(k, v, v_hi, v_lo, left, right):
                    c = k * v
                    return jnp.concatenate(
                        [c[:8] + right * v_hi, c[8 : COLS - 8], c[COLS - 8 :] + left * v_lo], 0
                    )

                own_rows.append(spread(mk[1], f, f_hi, f_lo, mk[0], mk[2]))
                far_rows.append(spread(kf[1], f, f_hi, f_lo, kf[0], kf[2]))
                own_g[0] += f_lo * bo[COLS - 8 :]
                own_g[1] += fold(f * bo)
                own_g[2] += f_hi * bo[:8]
                far_g[0] += f_lo * bf[COLS - 8 :]
                far_g[1] += fold(f * bf)
                far_g[2] += f_hi * bf[:8]
                bo_hi = pltpu.roll(bo[COLS - 8 :], 4, 0)
                bo_lo = pltpu.roll(bo[:8], 4, 0)
                bf_hi = pltpu.roll(bf[COLS - 8 :], 4, 0)
                bf_lo = pltpu.roll(bf[:8], 4, 0)
                g = mk[1] * bo + kf[1] * bf
                g_hi = jnp.where(low, mk[0] * bo_hi + kf[0] * bf_hi, 0.0)
                g_lo = jnp.where(low, 0.0, mk[2] * bo_lo + kf[2] * bf_lo)
                g = jnp.concatenate([g[:8] + g_hi, g[8 : COLS - 8], g[COLS - 8 :] + g_lo], 0)
                g = g.astype(BF16).astype(F32)
                shifted = [from_right(g), g, from_left(g)]
                for i in range(3):
                    for j in range(3):
                        first_acc[3 * i + j] += fold(x[r + i] * shifted[j])
            there = pl.ds(base, 2 * COLS)
            a_own[there, lanes] = jnp.concatenate(own_rows, 0).astype(BF16)
            a_far[there, lanes] = jnp.concatenate(far_rows, 0).astype(BF16)
            return tuple(first_acc), tuple(own_g), tuple(far_g)

        zero = jnp.zeros((8, LANES), F32)
        first_acc, own_g, far_g = lax.fori_loop(
            0, ROWS // 2, pair, ((zero,) * 9, (zero,) * 3, (zero,) * 3)
        )

        def line(v):
            return jnp.sum(v, axis=0, keepdims=True)

        far_lines = [line(v) for v in far_g]
        lines = [line(v) for v in first_acc]
        lines += [v * up_f for v in far_lines]
        lines += [line(v) for v in own_g]
        lines += [v * down_f for v in far_lines]
        lines.append(jnp.zeros((GRAD_ROWS - len(lines), LANES), F32))
        at = 2 * CHANNELS + (step * (BLOCK // LANES) + chunk) * GRAD_ROWS
        payload_ref[pl.ds(pl.multiple_of(at, GRAD_ROWS), GRAD_ROWS), :] = jnp.concatenate(
            lines, 0
        ).astype(BF16)

    own_acc[...] += jnp.dot(a_own[...], weights, preferred_element_type=F32)
    far_acc[...] += jnp.dot(a_far[...], weights, preferred_element_type=F32)
    part = lax.dot_general(a_own[...], weighted_ref[...], tn, preferred_element_type=F32)
    part += lax.dot_general(a_far[...], wfar[...], tn, preferred_element_type=F32)
    for half in range(WIDTH // LANES):
        at = pl.multiple_of(half * CHANNELS + step * BLOCK, BLOCK)
        payload_ref[pl.ds(at, BLOCK), :] = part[:, half * LANES : (half + 1) * LANES].astype(BF16)

    @pl.when(step == pl.num_programs(0) - 1)
    def _():
        own_out_ref[...] = own_acc[...]
        far_out_ref[...] = far_acc[...].astype(BF16)


def slab_work(slab, features, near, partner, weighted, first_kernel, holed_kernel, point_weight):
    whole = lambda shape: pl.BlockSpec(shape, lambda k, s: (0,) * len(shape))
    return pl.pallas_call(
        body,
        grid_spec=pltpu.PrefetchScalarGridSpec(
            num_scalar_prefetch=1,
            grid=(CHANNELS // BLOCK,),
            in_specs=[
                pl.BlockSpec((ROWS, COLS, BLOCK), lambda k, s: (0, 0, k)),
                pl.BlockSpec((COLS, BLOCK), lambda k, s: (0, k)),
                pl.BlockSpec((COLS, BLOCK), lambda k, s: (k, 0)),
                whole((CELLS, WIDTH)),
                whole((CELLS, WIDTH)),
                pl.BlockSpec((3, 3, BLOCK), lambda k, s: (0, 0, k)),
                pl.BlockSpec((3, 3, BLOCK), lambda k, s: (0, 0, k)),
                pl.BlockSpec((BLOCK, WIDTH), lambda k, s: (k, 0)),
            ],
            out_specs=[
                whole((PAYLOAD_ROWS, LANES)),
                whole((CELLS, WIDTH)),
                whole((CELLS, WIDTH)),
            ],
            scratch_shapes=[
                pltpu.VMEM(((ROWS + 2) * COLS, BLOCK), F32),
                pltpu.VMEM((CELLS, WIDTH), BF16),
                pltpu.VMEM((CELLS, BLOCK), F32),
                pltpu.VMEM((CELLS, BLOCK), F32),
                pltpu.VMEM((CELLS, BLOCK), BF16),
                pltpu.VMEM((CELLS, BLOCK), BF16),
                pltpu.VMEM((CELLS, WIDTH), F32),
                pltpu.VMEM((CELLS, WIDTH), F32),
            ],
        ),
        out_shape=[
            jax.ShapeDtypeStruct((PAYLOAD_ROWS, LANES), BF16),
            jax.ShapeDtypeStruct((CELLS, WIDTH), F32),
            jax.ShapeDtypeStruct((CELLS, WIDTH), BF16),
        ],
        compiler_params=pltpu.CompilerParams(vmem_limit_bytes=40 * 2**20),
        cost_estimate=pl.CostEstimate(
            flops=6 * 2 * CELLS * CHANNELS * WIDTH, bytes_accessed=6 * 2**20, transcendentals=0
        ),
    )(slab, features, near, partner, weighted, partner, first_kernel, holed_kernel, point_weight)


def per_device(features, labels, cotangent, first_kernel, holed_kernel, point_weight):
    count = lax.axis_size("dp")
    dims = {"z_lo": 4, "x": 4, "y": count // 16} if count >= 32 else {"z_lo": 1, "x": 1, "y": count}
    dims |= {"z_hi": 2, "core": 2}
    total = count * 4
    scale = 1.0 / math.sqrt(total * CELLS)
    slab = lax.axis_index("slab")
    core = slab % 2
    feats = features[0]

    label = labels.reshape(CELLS, 1)
    weighting = jnp.where(label == 0, 0.6, jnp.where(label == 1, 2.4, 1.5)).astype(F32)
    weighted = (cotangent.reshape(CELLS, WIDTH).astype(F32) * weighting).astype(BF16)

    row = jnp.where(core == 0, feats[ROWS - 1], feats[0])
    far_row = jnp.where(core == 0, feats[0], feats[ROWS - 1])
    packed = far_row.reshape(COLS, CHANNELS // BLOCK, BLOCK).transpose(1, 0, 2)
    packed = packed.reshape(CHANNELS // BLOCK * COLS, BLOCK)
    packed = jnp.pad(packed, ((0, CELLS - packed.shape[0]), (0, 0)))
    outer = (slab == 0) | (slab == 3)
    message = jnp.where(outer, weighted, packed)
    mirrored = [(d, d - d % 4 + 3 - d % 4) for d in range(total)]
    partner = lax.ppermute(message, AXES, mirrored)
    near = lax.ppermute(row, AXES, [(d, d ^ 1) for d in range(total)])

    payload, own, far = slab_work(
        slab[None].astype(jnp.int32),
        feats,
        near,
        partner,
        weighted,
        first_kernel,
        holed_kernel,
        point_weight,
    )
    arrived = lax.ppermute(far, AXES, [pair for pair in mirrored if pair[0] % 4 in (0, 3)])

    cores = device_groups(dims, "core")
    plane = device_groups(dims, "x", "z_hi", "z_lo")
    ring = device_groups(dims, "y")
    units = payload.reshape(-1, 8, LANES)
    units = scattered(units, cores).astype(BF16)
    units = scattered(units, plane).astype(BF16)
    parts = gathered(units, ring)
    units = (jnp.sum(parts.astype(F32), axis=0) * scale).astype(BF16)
    units = gathered(units, plane).reshape(-1, 8, LANES)
    result = gathered(units, cores).reshape(PAYLOAD_ROWS, LANES)

    branch_out = (own + arrived.astype(F32)).astype(BF16).reshape(1, ROWS, COLS, WIDTH)
    point_grad = jnp.concatenate([result[:CHANNELS], result[CHANNELS : 2 * CHANNELS]], axis=1)
    grads = result[2 * CHANNELS :].reshape(CHANNELS // LANES, GRAD_ROWS, LANES)[:, :18]
    grads = grads.transpose(1, 0, 2).astype(F32).reshape(2, 3, 3, CHANNELS)
    return (branch_out, point_grad, grads[0], grads[1])


def solution(mesh):
    in_specs = (
        P("dp", "slab", None, None),
        P("dp", "slab", None),
        P("dp", "slab", None, None),
        P(),
        P(),
        P(),
    )
    out_specs = (P("dp", "slab", None, None), P(), P(), P())
    return jax.shard_map(
        per_device, mesh=mesh, in_specs=in_specs, out_specs=out_specs, check_vma=False
    )
```

```python
import itertools
import math

import jax
import jax.numpy as jnp
from jax import lax
from jax.experimental import pallas as pl
from jax.experimental.pallas import tpu as pltpu
from jax.sharding import PartitionSpec as P

AXES = ("dp", "slab")
STEP = 36
ROWS = 12
COLS = 40
CELLS = ROWS * COLS
EDGE = COLS - STEP
CHANNELS = 2048
WIDTH = 256
BLOCK = 512
PACKED = 256
LANES = 128
GRAD_ROWS = 32
PAYLOAD_ROWS = 2 * CHANNELS + CHANNELS // LANES * GRAD_ROWS
F32 = jnp.float32
BF16 = jnp.bfloat16


def device_groups(dims, *names):
    strides, stride = {}, 1
    for name in reversed(dims):
        strides[name] = stride
        stride *= dims[name]

    def places(chosen):
        return [
            sum(i * strides[n] for n, i in zip(chosen, spot))
            for spot in itertools.product(*(range(dims[n]) for n in chosen))
        ]

    inside = places(names)
    return [[base + i for i in inside] for base in places([n for n in dims if n not in names])]


def exchange(parts, groups):
    return lax.all_to_all(parts, AXES, 0, 0, axis_index_groups=groups, tiled=True)


def scattered(units, groups):
    count = len(groups[0])
    parts = exchange(units.reshape(count, units.shape[0] // count, 8, LANES), groups)
    return jnp.sum(parts.astype(F32), axis=0)


def gathered(units, groups):
    count = len(groups[0])
    return exchange(jnp.broadcast_to(units[None], (count, *units.shape)), groups)


def widened(xs, x_ref, near, far, slab):
    core = lax.rem(slab, 2)
    one = jnp.where(core == 1, 1.0, 0.0)
    xs[pl.ds(0, COLS), :] = near * one + far * jnp.where(slab == 2, 1.0, 0.0)
    xs[pl.ds((ROWS + 1) * COLS, COLS), :] = near * (1.0 - one) + far * jnp.where(slab == 1, 1.0, 0.0)

    for r in range(ROWS):
        xs[pl.ds((r + 1) * COLS, COLS), :] = x_ref[r].astype(F32)


def from_left(v):
    sub = lax.broadcasted_iota(jnp.int32, (8, v.shape[1]), 0)
    moved = pltpu.roll(v, 1, 0)
    return jnp.concatenate([jnp.where(sub == 0, 0.0, moved[:8]), moved[8:]], 0)


def from_right(v):
    sub = lax.broadcasted_iota(jnp.int32, (8, v.shape[1]), 0)
    moved = pltpu.roll(v, COLS - 1, 0)
    return jnp.concatenate([moved[: COLS - 8], jnp.where(sub == 7, 0.0, moved[COLS - 8 :])], 0)


def fold(v):
    parts = [v[8 * i : 8 * i + 8] for i in range(COLS // 8)]
    while len(parts) > 1:
        parts = [a + b for a, b in zip(parts[::2], parts[1::2])] + (
            parts[-1:] if len(parts) % 2 else []
        )
    return parts[0]


def conv_row(fk, x):
    side = [fk[0][j] * x[0] + fk[1][j] * x[1] + fk[2][j] * x[2] for j in range(3)]
    return side[1] + from_left(side[0]) + from_right(side[2])


def ends(v):
    low = lax.broadcasted_iota(jnp.int32, (8, LANES), 0) < EDGE
    high_end = jnp.where(low, pltpu.roll(v[COLS - 8 :], 4, 0), 0.0)
    low_end = jnp.where(low, 0.0, pltpu.roll(v[:8], 4, 0))
    return high_end, low_end


def spread(k, v, v_ends):
    c = k[1] * v
    return jnp.concatenate(
        [c[:8] + k[2] * v_ends[0], c[8 : COLS - 8], c[COLS - 8 :] + k[0] * v_ends[1]], 0
    )


def taps(ref, lanes):
    return [[ref[i, j : j + 1, lanes] for j in range(3)] for i in range(3)]


def far_taps(hk, slab):
    up = jnp.where(slab == 0, 1.0, 0.0)
    down = jnp.where(slab == 3, 1.0, 0.0)
    return [hk[0][j] * up + hk[2][j] * down for j in range(3)]


def first_body(
    slab_ref, x_ref, near_ref, first_k_ref, holed_k_ref, point_ref, f_ref, far_out_ref, xs, a_far, far_acc
):
    step = pl.program_id(0)
    slab = slab_ref[0]

    @pl.when(step == 0)
    def _():
        far_acc[...] = jnp.zeros_like(far_acc)

    widened(xs, x_ref, near_ref[...].astype(F32), jnp.zeros((COLS, BLOCK), F32), slab)
    for chunk in range(BLOCK // LANES):
        lanes = pl.ds(chunk * LANES, LANES)
        fk = taps(first_k_ref, lanes)
        kf = far_taps(taps(holed_k_ref, lanes), slab)

        for p in range(ROWS // 2):
            base = p * 2 * COLS
            x = [xs[pl.ds(base + i * COLS, COLS), lanes] for i in range(4)]
            far_rows = []
            for r in range(2):
                f16 = conv_row(fk, x[r : r + 3]).astype(BF16)
                f_ref[2 * p + r, :, lanes] = f16
                f = f16.astype(F32)
                far_rows.append(spread(kf, f, ends(f)))
            a_far[pl.ds(base, 2 * COLS), lanes] = jnp.concatenate(far_rows, 0).astype(BF16)

    far_acc[...] += jnp.dot(a_far[...], point_ref[...], preferred_element_type=F32)

    @pl.when(step == pl.num_programs(0) - 1)
    def _():
        far_out_ref[...] = far_acc[...].astype(BF16)


def second_body(
    slab_ref,
    x_ref,
    near_ref,
    far_ref,
    weighted_ref,
    partner_ref,
    f_ref,
    first_k_ref,
    holed_k_ref,
    point_ref,
    payload_ref,
    own_out_ref,
    xs,
    wfar,
    b_own,
    b_far,
    a_own,
    a_far,
    f_edge,
    own_acc,
):
    step = pl.program_id(0)
    slab = slab_ref[0]
    edge = jnp.where(lax.rem(slab, 2) == 0, 0, ROWS - 1)
    up = jnp.where(slab == 0, 1.0, 0.0)
    down = jnp.where(slab == 3, 1.0, 0.0)

    @pl.when(step == 0)
    def _():
        wfar[...] = (partner_ref[...].astype(F32) * (up + down)).astype(BF16)
        own_acc[...] = jnp.zeros_like(own_acc)

    far = far_ref[...].astype(F32)
    far = jnp.concatenate([far[i * COLS : (i + 1) * COLS] for i in range(BLOCK // PACKED)], 1)
    widened(xs, x_ref, near_ref[...].astype(F32), far, slab)

    weights = point_ref[...]
    nt = (((1,), (1,)), ((), ()))
    tn = (((0,), (0,)), ((), ()))
    for given, back in ((weighted_ref, b_own), (wfar, b_far)):
        product = lax.dot_general(given[...], weights, nt, preferred_element_type=F32)
        back[...] = product.astype(BF16).astype(F32)

    for chunk in range(BLOCK // LANES):
        lanes = pl.ds(chunk * LANES, LANES)
        fk = taps(first_k_ref, lanes)
        hk = taps(holed_k_ref, lanes)
        mk = hk[1]
        kf = far_taps(hk, slab)
        x = [xs[pl.ds(pl.multiple_of((edge + i) * COLS, 8), COLS), lanes] for i in range(3)]
        f_edge[...] = conv_row(fk, x).astype(BF16).astype(F32)

        zero = jnp.zeros((8, LANES), F32)
        first_acc, own_g, far_g = [zero] * 9, [zero] * 3, [zero] * 3
        for p in range(ROWS // 2):
            base = p * 2 * COLS
            own_rows, far_rows = [], []
            for r in range(2):
                here = pl.ds(base + r * COLS, COLS)
                f = f_ref[2 * p + r, :, lanes].astype(F32)
                if 2 * p + r in (0, ROWS - 1):
                    f = jnp.where(2 * p + r == edge, f_edge[...], f)
                bo, bf = b_own[here, lanes], b_far[here, lanes]
                f_ends = ends(f)
                own_rows.append(spread(mk, f, f_ends))
                far_rows.append(spread(kf, f, f_ends))
                for sums, b in ((own_g, bo), (far_g, bf)):
                    sums[0] += f_ends[1] * b[COLS - 8 :]
                    sums[1] += fold(f * b)
                    sums[2] += f_ends[0] * b[:8]
                bo_ends, bf_ends = ends(bo), ends(bf)
                g = spread(mk[::-1], bo, bo_ends) + spread(kf[::-1], bf, bf_ends)
                g = g.astype(BF16).astype(F32)
                shifted = [from_right(g), g, from_left(g)]
                for i in range(3):
                    x = xs[pl.ds(base + (r + i) * COLS, COLS), lanes]
                    for j in range(3):
                        first_acc[3 * i + j] += fold(x * shifted[j])
            there = pl.ds(base, 2 * COLS)
            a_own[there, lanes] = jnp.concatenate(own_rows, 0).astype(BF16)
            a_far[there, lanes] = jnp.concatenate(far_rows, 0).astype(BF16)

        def line(v):
            return jnp.sum(v, axis=0, keepdims=True)

        far_lines = [line(v) for v in far_g]
        lines = [line(v) for v in first_acc]
        lines += [v * up for v in far_lines]
        lines += [line(v) for v in own_g]
        lines += [v * down for v in far_lines]
        lines.append(jnp.zeros((GRAD_ROWS - len(lines), LANES), F32))
        at = 2 * CHANNELS + (step * (BLOCK // LANES) + chunk) * GRAD_ROWS
        payload_ref[pl.ds(pl.multiple_of(at, GRAD_ROWS), GRAD_ROWS), :] = jnp.concatenate(
            lines, 0
        ).astype(BF16)

    own_acc[...] += jnp.dot(a_own[...], weights, preferred_element_type=F32)
    part = lax.dot_general(a_own[...], weighted_ref[...], tn, preferred_element_type=F32)
    part += lax.dot_general(a_far[...], wfar[...], tn, preferred_element_type=F32)
    for half in range(WIDTH // LANES):
        at = pl.multiple_of(half * CHANNELS + step * BLOCK, BLOCK)
        payload_ref[pl.ds(at, BLOCK), :] = part[:, half * LANES : (half + 1) * LANES].astype(BF16)

    @pl.when(step == pl.num_programs(0) - 1)
    def _():
        own_out_ref[...] = own_acc[...]


def whole(shape):
    return pl.BlockSpec(shape, lambda k, s: (0,) * len(shape))


def kernel_call(body, in_specs, out_specs, out_shape, scratch_shapes, flops):
    return pl.pallas_call(
        body,
        grid_spec=pltpu.PrefetchScalarGridSpec(
            num_scalar_prefetch=1,
            grid=(CHANNELS // BLOCK,),
            in_specs=in_specs,
            out_specs=out_specs,
            scratch_shapes=scratch_shapes,
        ),
        out_shape=out_shape,
        compiler_params=pltpu.CompilerParams(vmem_limit_bytes=40 * 2**20),
        cost_estimate=pl.CostEstimate(flops=flops, bytes_accessed=8 * 2**20, transcendentals=0),
    )


SLAB_SPEC = pl.BlockSpec((ROWS, COLS, BLOCK), lambda k, s: (0, 0, k))
LINE_SPEC = pl.BlockSpec((COLS, BLOCK), lambda k, s: (0, k))
TAPS_SPEC = pl.BlockSpec((3, 3, BLOCK), lambda k, s: (0, 0, k))
POINT_SPEC = pl.BlockSpec((BLOCK, WIDTH), lambda k, s: (k, 0))
CELLS_SPEC = whole((CELLS, WIDTH))


def first_work(slab, features, near, first_kernel, holed_kernel, point_weight):
    return kernel_call(
        first_body,
        [SLAB_SPEC, LINE_SPEC, TAPS_SPEC, TAPS_SPEC, POINT_SPEC],
        [SLAB_SPEC, CELLS_SPEC],
        [
            jax.ShapeDtypeStruct((ROWS, COLS, CHANNELS), BF16),
            jax.ShapeDtypeStruct((CELLS, WIDTH), BF16),
        ],
        [
            pltpu.VMEM(((ROWS + 2) * COLS, BLOCK), F32),
            pltpu.VMEM((CELLS, BLOCK), BF16),
            pltpu.VMEM((CELLS, WIDTH), F32),
        ],
        2 * 2 * CELLS * CHANNELS * WIDTH,
    )(slab, features, near, first_kernel, holed_kernel, point_weight)


def second_work(slab, features, near, partner, weighted, first, first_kernel, holed_kernel, point_weight):
    packs = BLOCK // PACKED
    return kernel_call(
        second_body,
        [
            SLAB_SPEC,
            LINE_SPEC,
            pl.BlockSpec((packs * COLS, PACKED), lambda k, s: (k, 0)),
            CELLS_SPEC,
            CELLS_SPEC,
            SLAB_SPEC,
            TAPS_SPEC,
            TAPS_SPEC,
            POINT_SPEC,
        ],
        [whole((PAYLOAD_ROWS, LANES)), CELLS_SPEC],
        [
            jax.ShapeDtypeStruct((PAYLOAD_ROWS, LANES), BF16),
            jax.ShapeDtypeStruct((CELLS, WIDTH), F32),
        ],
        [
            pltpu.VMEM(((ROWS + 2) * COLS, BLOCK), F32),
            pltpu.VMEM((CELLS, WIDTH), BF16),
            pltpu.VMEM((CELLS, BLOCK), F32),
            pltpu.VMEM((CELLS, BLOCK), F32),
            pltpu.VMEM((CELLS, BLOCK), BF16),
            pltpu.VMEM((CELLS, BLOCK), BF16),
            pltpu.VMEM((COLS, LANES), F32),
            pltpu.VMEM((CELLS, WIDTH), F32),
        ],
        10 * 2 * CELLS * CHANNELS * WIDTH,
    )(
        slab,
        features,
        near,
        partner,
        weighted,
        partner,
        first,
        first_kernel,
        holed_kernel,
        point_weight,
    )


def prepare_body(slab_ref, label_ref, cot_ref, near_ref, far_ref, row_ref, message_ref, weighted_ref):
    slab = slab_ref[0]
    outer = jnp.logical_or(slab == 0, slab == 3)
    row_ref[...] = near_ref[0]
    diagonal = lax.broadcasted_iota(jnp.int32, (COLS, COLS), 0) == lax.broadcasted_iota(
        jnp.int32, (COLS, COLS), 1
    )
    for p in range(ROWS // 2):
        pair = pl.ds(2 * COLS * p, 2 * COLS)
        columns = []
        for r in range(2 * p, 2 * p + 2):
            label = label_ref[r]
            weight = jnp.where(label == 0, 0.6, jnp.where(label == 1, 2.4, 1.5)).astype(F32)
            spot = jnp.where(diagonal, jnp.broadcast_to(weight, (COLS, COLS)), 0.0)
            columns.append(jnp.sum(spot, axis=1, keepdims=True))
        scaled = (cot_ref[pair, :].astype(F32) * jnp.concatenate(columns, 0)).astype(BF16)
        weighted_ref[pair, :] = scaled

    @pl.when(outer)
    def _():
        message_ref[...] = weighted_ref[...]

    @pl.when(jnp.logical_not(outer))
    def _():
        packs = CHANNELS // PACKED
        for q in range(0, packs, 2):
            two = [far_ref[0, :, (q + i) * PACKED : (q + i + 1) * PACKED].astype(F32) for i in range(2)]
            message_ref[pl.ds(q * COLS, 2 * COLS), :] = jnp.concatenate(two, 0).astype(BF16)
        rest = CELLS - packs * COLS
        message_ref[pl.ds(packs * COLS, rest), :] = jnp.zeros((rest, WIDTH), BF16)


def prepare(slab, features, labels, cotangent):
    def edge_row(far):
        last = lambda s: (ROWS - 1) * lax.rem(s[0] + 1 - far, 2)
        return pl.BlockSpec((1, COLS, CHANNELS), lambda k, s: (last(s), 0, 0))

    cells = jax.ShapeDtypeStruct((CELLS, WIDTH), BF16)
    return pl.pallas_call(
        prepare_body,
        grid_spec=pltpu.PrefetchScalarGridSpec(
            num_scalar_prefetch=1,
            grid=(1,),
            in_specs=[whole((ROWS, 1, COLS)), CELLS_SPEC, edge_row(0), edge_row(1)],
            out_specs=[whole((COLS, CHANNELS)), CELLS_SPEC, CELLS_SPEC],
        ),
        out_shape=[jax.ShapeDtypeStruct((COLS, CHANNELS), BF16), cells, cells],
        compiler_params=pltpu.CompilerParams(vmem_limit_bytes=56 * 2**20),
    )(slab, labels, cotangent, features, features)


def finish_body(left_ref, right_ref, lines_ref, point_ref, first_ref, atrous_ref):
    point_ref[:, :LANES] = left_ref[...]
    point_ref[:, LANES:] = right_ref[...]

    @pl.when(pl.program_id(0) == 0)
    def _():
        for q in range(CHANNELS // LANES):
            lanes = pl.ds(q * LANES, LANES)
            lines = lines_ref[pl.ds(q * GRAD_ROWS, GRAD_ROWS), :].astype(F32)
            for i in range(3):
                first_ref[i, :, lanes] = lines[3 * i : 3 * i + 3]
                atrous_ref[i, :, lanes] = lines[9 + 3 * i : 12 + 3 * i]


def finish(result):
    steps = 4
    block = CHANNELS // steps
    taps_shape = jax.ShapeDtypeStruct((3, 3, CHANNELS), F32)
    taps_spec = pl.BlockSpec((3, 3, CHANNELS), lambda k: (0, 0, 0))
    return pl.pallas_call(
        finish_body,
        grid=(steps,),
        in_specs=[
            pl.BlockSpec((block, LANES), lambda k: (k, 0)),
            pl.BlockSpec((block, LANES), lambda k: (k + steps, 0)),
            pl.BlockSpec((block, LANES), lambda k: (2 * steps, 0)),
        ],
        out_specs=[pl.BlockSpec((block, WIDTH), lambda k: (k, 0)), taps_spec, taps_spec],
        out_shape=[jax.ShapeDtypeStruct((CHANNELS, WIDTH), BF16), taps_shape, taps_shape],
        compiler_params=pltpu.CompilerParams(vmem_limit_bytes=16 * 2**20),
    )(result, result, result)


def per_device(features, labels, cotangent, first_kernel, holed_kernel, point_weight):
    count = lax.axis_size("dp")
    wide = count >= 32
    dims = {"z_mid": 2 if wide else 1, "z_low": 2 if wide else 1, "x": 4 if wide else 1}
    dims |= {"y_high": count // 32 if wide else 1, "y_low": 2, "z_top": 2, "core": 2}
    total = count * 4
    scale = 1.0 / math.sqrt(total * CELLS)
    slab = lax.axis_index("slab")
    where = slab[None].astype(jnp.int32)
    feats = features[0]
    row, message, weighted = prepare(
        where, feats, labels.reshape(ROWS, 1, COLS), cotangent.reshape(CELLS, WIDTH)
    )
    mirrored = [(d, d - d % 4 + 3 - d % 4) for d in range(total)]
    partner = lax.ppermute(message, AXES, mirrored)
    near = lax.ppermute(row, AXES, [(d, d ^ 1) for d in range(total)])

    first, far = first_work(where, feats, near, first_kernel, holed_kernel, point_weight)
    arrived = lax.ppermute(far, AXES, [pair for pair in mirrored if pair[0] % 4 in (0, 3)])

    payload, own = second_work(
        where, feats, near, partner, weighted, first, first_kernel, holed_kernel, point_weight
    )

    cores = device_groups(dims, "core")
    block = device_groups(dims, "z_low", "x", "y_low")
    z_ring = device_groups(dims, "z_top", "z_mid")
    y_ring = device_groups(dims, "y_high")
    units = payload.reshape(-1, 8, LANES)
    units = scattered(units, cores).astype(BF16)
    units, arrived = lax.optimization_barrier((units, arrived))
    units = scattered(units, block).astype(BF16)
    units = jnp.sum(gathered(units, z_ring).astype(F32), axis=0).astype(BF16)
    units = (jnp.sum(gathered(units, y_ring).astype(F32), axis=0) * scale).astype(BF16)
    units = gathered(units, block).reshape(-1, 8, LANES)
    result = gathered(units, cores).reshape(PAYLOAD_ROWS, LANES)

    branch_out = (own + arrived.astype(F32)).astype(BF16).reshape(1, ROWS, COLS, WIDTH)
    point_grad, first_grad, atrous_grad = finish(result)
    return (branch_out, point_grad, first_grad, atrous_grad)


def solution(mesh):
    in_specs = (
        P("dp", "slab", None, None),
        P("dp", "slab", None),
        P("dp", "slab", None, None),
        P(),
        P(),
        P(),
    )
    out_specs = (P("dp", "slab", None, None), P(), P(), P())
    return jax.shard_map(
        per_device, mesh=mesh, in_specs=in_specs, out_specs=out_specs, check_vma=False
    )
```

```python
import itertools
import math

import jax
import jax.numpy as jnp
from jax import lax
from jax.experimental import pallas as pl
from jax.experimental.pallas import tpu as pltpu
from jax.sharding import PartitionSpec as P

AXES = ("dp", "slab")
STEP = 36
ROWS = 12
COLS = 40
CELLS = ROWS * COLS
EDGE = COLS - STEP
CHANNELS = 2048
WIDTH = 256
BLOCK = 512
PACKED = 256
LANES = 128
GRAD_ROWS = 32
HALF = CHANNELS // 2
PAYLOAD_ROWS = 2 * HALF + HALF // LANES * GRAD_ROWS
F32 = jnp.float32
BF16 = jnp.bfloat16


def device_groups(dims, *names):
    strides, stride = {}, 1
    for name in reversed(dims):
        strides[name] = stride
        stride *= dims[name]

    def places(chosen):
        return [
            sum(i * strides[n] for n, i in zip(chosen, spot))
            for spot in itertools.product(*(range(dims[n]) for n in chosen))
        ]

    inside = places(names)
    return [[base + i for i in inside] for base in places([n for n in dims if n not in names])]


def exchange(parts, groups):
    return lax.all_to_all(parts, AXES, 0, 0, axis_index_groups=groups, tiled=True)


def scattered(units, groups):
    count = len(groups[0])
    parts = exchange(units.reshape(count, units.shape[0] // count, 8, LANES), groups)
    return jnp.sum(parts.astype(F32), axis=0)


def gathered(units, groups):
    count = len(groups[0])
    return exchange(jnp.broadcast_to(units[None], (count, *units.shape)), groups)


def widened(xs, x_ref, near, far, slab):
    core = lax.rem(slab, 2)
    one = jnp.where(core == 1, 1.0, 0.0)
    xs[pl.ds(0, COLS), :] = near * one + far * jnp.where(slab == 2, 1.0, 0.0)
    xs[pl.ds((ROWS + 1) * COLS, COLS), :] = near * (1.0 - one) + far * jnp.where(slab == 1, 1.0, 0.0)

    for r in range(ROWS):
        xs[pl.ds((r + 1) * COLS, COLS), :] = x_ref[r].astype(F32)


def from_left(v):
    sub = lax.broadcasted_iota(jnp.int32, (8, v.shape[1]), 0)
    moved = pltpu.roll(v, 1, 0)
    return jnp.concatenate([jnp.where(sub == 0, 0.0, moved[:8]), moved[8:]], 0)


def from_right(v):
    sub = lax.broadcasted_iota(jnp.int32, (8, v.shape[1]), 0)
    moved = pltpu.roll(v, COLS - 1, 0)
    return jnp.concatenate([moved[: COLS - 8], jnp.where(sub == 7, 0.0, moved[COLS - 8 :])], 0)


def fold(v):
    parts = [v[8 * i : 8 * i + 8] for i in range(COLS // 8)]
    while len(parts) > 1:
        parts = [a + b for a, b in zip(parts[::2], parts[1::2])] + (
            parts[-1:] if len(parts) % 2 else []
        )
    return parts[0]


def conv_row(fk, x):
    side = [fk[0][j] * x[0] + fk[1][j] * x[1] + fk[2][j] * x[2] for j in range(3)]
    return side[1] + from_left(side[0]) + from_right(side[2])


def ends(v):
    low = lax.broadcasted_iota(jnp.int32, (8, LANES), 0) < EDGE
    high_end = jnp.where(low, pltpu.roll(v[COLS - 8 :], 4, 0), 0.0)
    low_end = jnp.where(low, 0.0, pltpu.roll(v[:8], 4, 0))
    return high_end, low_end


def spread(k, v, v_ends):
    c = k[1] * v
    return jnp.concatenate(
        [c[:8] + k[2] * v_ends[0], c[8 : COLS - 8], c[COLS - 8 :] + k[0] * v_ends[1]], 0
    )


def taps(ref, lanes):
    return [[ref[i, j : j + 1, lanes] for j in range(3)] for i in range(3)]


def far_taps(hk, slab):
    up = jnp.where(slab == 0, 1.0, 0.0)
    down = jnp.where(slab == 3, 1.0, 0.0)
    return [hk[0][j] * up + hk[2][j] * down for j in range(3)]


def first_body(
    slab_ref, x_ref, near_ref, first_k_ref, holed_k_ref, point_ref, f_ref, far_out_ref, xs, a_far, far_acc
):
    step = pl.program_id(0)
    slab = slab_ref[0]

    @pl.when(step == 0)
    def _():
        far_acc[...] = jnp.zeros_like(far_acc)

    widened(xs, x_ref, near_ref[...].astype(F32), jnp.zeros((COLS, BLOCK), F32), slab)
    for chunk in range(BLOCK // LANES):
        lanes = pl.ds(chunk * LANES, LANES)
        fk = taps(first_k_ref, lanes)
        kf = far_taps(taps(holed_k_ref, lanes), slab)

        for p in range(ROWS // 2):
            base = p * 2 * COLS
            x = [xs[pl.ds(base + i * COLS, COLS), lanes] for i in range(4)]
            far_rows = []
            for r in range(2):
                f16 = conv_row(fk, x[r : r + 3]).astype(BF16)
                f_ref[2 * p + r, :, lanes] = f16
                f = f16.astype(F32)
                far_rows.append(spread(kf, f, ends(f)))
            a_far[pl.ds(base, 2 * COLS), lanes] = jnp.concatenate(far_rows, 0).astype(BF16)

    far_acc[...] += jnp.dot(a_far[...], point_ref[...], preferred_element_type=F32)

    @pl.when(step == pl.num_programs(0) - 1)
    def _():
        far_out_ref[...] = far_acc[...].astype(BF16)


def second_body(
    slab_ref,
    x_ref,
    near_ref,
    far_ref,
    weighted_ref,
    partner_ref,
    f_ref,
    first_k_ref,
    holed_k_ref,
    point_ref,
    payload_ref,
    own_out_ref,
    xs,
    wfar,
    b_own,
    b_far,
    a_own,
    a_far,
    f_edge,
    own_acc,
):
    step = pl.program_id(0)
    slab = slab_ref[0]
    edge = jnp.where(lax.rem(slab, 2) == 0, 0, ROWS - 1)
    up = jnp.where(slab == 0, 1.0, 0.0)
    down = jnp.where(slab == 3, 1.0, 0.0)

    @pl.when(step == 0)
    def _():
        wfar[...] = (partner_ref[...].astype(F32) * (up + down)).astype(BF16)
        own_acc[...] = jnp.zeros_like(own_acc)

    far = far_ref[...].astype(F32)
    far = jnp.concatenate([far[i * COLS : (i + 1) * COLS] for i in range(BLOCK // PACKED)], 1)
    widened(xs, x_ref, near_ref[...].astype(F32), far, slab)

    weights = point_ref[...]
    nt = (((1,), (1,)), ((), ()))
    tn = (((0,), (0,)), ((), ()))
    for given, back in ((weighted_ref, b_own), (wfar, b_far)):
        product = lax.dot_general(given[...], weights, nt, preferred_element_type=F32)
        back[...] = product.astype(BF16).astype(F32)

    for chunk in range(BLOCK // LANES):
        lanes = pl.ds(chunk * LANES, LANES)
        fk = taps(first_k_ref, lanes)
        hk = taps(holed_k_ref, lanes)
        mk = hk[1]
        kf = far_taps(hk, slab)
        x = [xs[pl.ds(pl.multiple_of((edge + i) * COLS, 8), COLS), lanes] for i in range(3)]
        f_edge[...] = conv_row(fk, x).astype(BF16).astype(F32)

        zero = jnp.zeros((8, LANES), F32)
        first_acc, own_g, far_g = [zero] * 9, [zero] * 3, [zero] * 3
        for p in range(ROWS // 2):
            base = p * 2 * COLS
            own_rows, far_rows = [], []
            for r in range(2):
                here = pl.ds(base + r * COLS, COLS)
                f = f_ref[2 * p + r, :, lanes].astype(F32)
                if 2 * p + r in (0, ROWS - 1):
                    f = jnp.where(2 * p + r == edge, f_edge[...], f)
                bo, bf = b_own[here, lanes], b_far[here, lanes]
                f_ends = ends(f)
                own_rows.append(spread(mk, f, f_ends))
                far_rows.append(spread(kf, f, f_ends))
                for sums, b in ((own_g, bo), (far_g, bf)):
                    sums[0] += f_ends[1] * b[COLS - 8 :]
                    sums[1] += fold(f * b)
                    sums[2] += f_ends[0] * b[:8]
                bo_ends, bf_ends = ends(bo), ends(bf)
                g = spread(mk[::-1], bo, bo_ends) + spread(kf[::-1], bf, bf_ends)
                g = g.astype(BF16).astype(F32)
                shifted = [from_right(g), g, from_left(g)]
                for i in range(3):
                    x = xs[pl.ds(base + (r + i) * COLS, COLS), lanes]
                    for j in range(3):
                        first_acc[3 * i + j] += fold(x * shifted[j])
            there = pl.ds(base, 2 * COLS)
            a_own[there, lanes] = jnp.concatenate(own_rows, 0).astype(BF16)
            a_far[there, lanes] = jnp.concatenate(far_rows, 0).astype(BF16)

        def line(v):
            return jnp.sum(v, axis=0, keepdims=True)

        far_lines = [line(v) for v in far_g]
        lines = [line(v) for v in first_acc]
        lines += [v * up for v in far_lines]
        lines += [line(v) for v in own_g]
        lines += [v * down for v in far_lines]
        lines.append(jnp.zeros((GRAD_ROWS - len(lines), LANES), F32))
        at = 2 * HALF + (step * (BLOCK // LANES) + chunk) * GRAD_ROWS
        payload_ref[pl.ds(pl.multiple_of(at, GRAD_ROWS), GRAD_ROWS), :] = jnp.concatenate(
            lines, 0
        ).astype(BF16)

    own_acc[...] += jnp.dot(a_own[...], weights, preferred_element_type=F32)
    part = lax.dot_general(a_own[...], weighted_ref[...], tn, preferred_element_type=F32)
    part += lax.dot_general(a_far[...], wfar[...], tn, preferred_element_type=F32)
    for half in range(WIDTH // LANES):
        at = pl.multiple_of(half * HALF + step * BLOCK, BLOCK)
        payload_ref[pl.ds(at, BLOCK), :] = part[:, half * LANES : (half + 1) * LANES].astype(BF16)

    @pl.when(step == pl.num_programs(0) - 1)
    def _():
        own_out_ref[...] = own_acc[...]


def whole(shape):
    return pl.BlockSpec(shape, lambda k, s: (0,) * len(shape))


def kernel_call(body, steps, in_specs, out_specs, out_shape, scratch_shapes, flops):
    return pl.pallas_call(
        body,
        grid_spec=pltpu.PrefetchScalarGridSpec(
            num_scalar_prefetch=1,
            grid=(steps,),
            in_specs=in_specs,
            out_specs=out_specs,
            scratch_shapes=scratch_shapes,
        ),
        out_shape=out_shape,
        compiler_params=pltpu.CompilerParams(vmem_limit_bytes=40 * 2**20),
        cost_estimate=pl.CostEstimate(flops=flops, bytes_accessed=8 * 2**20, transcendentals=0),
    )


def channel_specs(at):
    return (
        pl.BlockSpec((ROWS, COLS, BLOCK), lambda k, s: (0, 0, at(k, s))),
        pl.BlockSpec((COLS, BLOCK), lambda k, s: (0, at(k, s))),
        pl.BlockSpec((3, 3, BLOCK), lambda k, s: (0, 0, at(k, s))),
        pl.BlockSpec((BLOCK, WIDTH), lambda k, s: (at(k, s), 0)),
    )


CELLS_SPEC = whole((CELLS, WIDTH))


def first_work(slab, features, near, first_kernel, holed_kernel, point_weight):
    slab_spec, line_spec, taps_spec, point_spec = channel_specs(lambda k, s: k)
    return kernel_call(
        first_body,
        CHANNELS // BLOCK,
        [slab_spec, line_spec, taps_spec, taps_spec, point_spec],
        [slab_spec, CELLS_SPEC],
        [
            jax.ShapeDtypeStruct((ROWS, COLS, CHANNELS), BF16),
            jax.ShapeDtypeStruct((CELLS, WIDTH), BF16),
        ],
        [
            pltpu.VMEM(((ROWS + 2) * COLS, BLOCK), F32),
            pltpu.VMEM((CELLS, BLOCK), BF16),
            pltpu.VMEM((CELLS, WIDTH), F32),
        ],
        2 * 2 * CELLS * CHANNELS * WIDTH,
    )(slab, features, near, first_kernel, holed_kernel, point_weight)


def second_work(
    other, slab, features, near, partner, weighted, first, first_kernel, holed_kernel, point_weight
):
    packs = BLOCK // PACKED
    steps = HALF // BLOCK
    at = lambda k, s: k + steps * lax.rem(s[0] + other, 2)
    slab_spec, line_spec, taps_spec, point_spec = channel_specs(at)
    return kernel_call(
        second_body,
        steps,
        [
            slab_spec,
            line_spec,
            pl.BlockSpec((packs * COLS, PACKED), lambda k, s: (at(k, s), 0)),
            CELLS_SPEC,
            CELLS_SPEC,
            slab_spec,
            taps_spec,
            taps_spec,
            point_spec,
        ],
        [whole((PAYLOAD_ROWS, LANES)), CELLS_SPEC],
        [
            jax.ShapeDtypeStruct((PAYLOAD_ROWS, LANES), BF16),
            jax.ShapeDtypeStruct((CELLS, WIDTH), F32),
        ],
        [
            pltpu.VMEM(((ROWS + 2) * COLS, BLOCK), F32),
            pltpu.VMEM((CELLS, WIDTH), BF16),
            pltpu.VMEM((CELLS, BLOCK), F32),
            pltpu.VMEM((CELLS, BLOCK), F32),
            pltpu.VMEM((CELLS, BLOCK), BF16),
            pltpu.VMEM((CELLS, BLOCK), BF16),
            pltpu.VMEM((COLS, LANES), F32),
            pltpu.VMEM((CELLS, WIDTH), F32),
        ],
        1000 * 2 * CELLS * HALF * WIDTH,
    )(
        slab,
        features,
        near,
        partner,
        weighted,
        partner,
        first,
        first_kernel,
        holed_kernel,
        point_weight,
    )


def prepare_body(slab_ref, label_ref, cot_ref, far_ref, _, message_ref, weighted_ref):
    slab = slab_ref[0]
    outer = jnp.logical_or(slab == 0, slab == 3)
    diagonal = lax.broadcasted_iota(jnp.int32, (COLS, COLS), 0) == lax.broadcasted_iota(
        jnp.int32, (COLS, COLS), 1
    )
    for p in range(ROWS // 2):
        pair = pl.ds(2 * COLS * p, 2 * COLS)
        columns = []
        for r in range(2 * p, 2 * p + 2):
            label = label_ref[r]
            weight = jnp.where(label == 0, 0.6, jnp.where(label == 1, 2.4, 1.5)).astype(F32)
            spot = jnp.where(diagonal, jnp.broadcast_to(weight, (COLS, COLS)), 0.0)
            columns.append(jnp.sum(spot, axis=1, keepdims=True))
        scaled = (cot_ref[pair, :].astype(F32) * jnp.concatenate(columns, 0)).astype(BF16)
        weighted_ref[pair, :] = scaled

    @pl.when(outer)
    def _():
        message_ref[...] = weighted_ref[...]

    @pl.when(jnp.logical_not(outer))
    def _():
        packs = CHANNELS // PACKED
        for q in range(0, packs, 2):
            two = [far_ref[0, :, (q + i) * PACKED : (q + i + 1) * PACKED].astype(F32) for i in range(2)]
            message_ref[pl.ds(q * COLS, 2 * COLS), :] = jnp.concatenate(two, 0).astype(BF16)
        rest = CELLS - packs * COLS
        message_ref[pl.ds(packs * COLS, rest), :] = jnp.zeros((rest, WIDTH), BF16)


def prepare(slab, features, labels, cotangent, weights):
    far_row = pl.BlockSpec((1, COLS, CHANNELS), lambda k, s: ((ROWS - 1) * lax.rem(s[0], 2), 0, 0))
    cells = jax.ShapeDtypeStruct((CELLS, WIDTH), BF16)
    return pl.pallas_call(
        prepare_body,
        grid_spec=pltpu.PrefetchScalarGridSpec(
            num_scalar_prefetch=1,
            grid=(1,),
            in_specs=[whole((ROWS, 1, COLS)), CELLS_SPEC, far_row, whole((16, WIDTH))],
            out_specs=[CELLS_SPEC, CELLS_SPEC],
        ),
        out_shape=[cells, cells],
        compiler_params=pltpu.CompilerParams(vmem_limit_bytes=56 * 2**20),
    )(slab, labels, cotangent, features, weights)


def finish_body(half_ref, point_ref, first_ref, atrous_ref):
    point_ref[:, :LANES] = half_ref[:HALF, :]
    point_ref[:, LANES:] = half_ref[HALF : 2 * HALF, :]
    for q in range(HALF // LANES):
        lanes = pl.ds(pl.multiple_of(pl.program_id(0) * HALF + q * LANES, LANES), LANES)
        lines = half_ref[2 * HALF + q * GRAD_ROWS : 2 * HALF + (q + 1) * GRAD_ROWS, :].astype(F32)
        for i in range(3):
            first_ref[i, :, lanes] = lines[3 * i : 3 * i + 3]
            atrous_ref[i, :, lanes] = lines[9 + 3 * i : 12 + 3 * i]


def finish(result):
    taps_shape = jax.ShapeDtypeStruct((3, 3, CHANNELS), F32)
    taps_spec = pl.BlockSpec((3, 3, CHANNELS), lambda k: (0, 0, 0))
    return pl.pallas_call(
        finish_body,
        grid=(2,),
        in_specs=[pl.BlockSpec((PAYLOAD_ROWS, LANES), lambda k: (k, 0))],
        out_specs=[pl.BlockSpec((HALF, WIDTH), lambda k: (k, 0)), taps_spec, taps_spec],
        out_shape=[jax.ShapeDtypeStruct((CHANNELS, WIDTH), BF16), taps_shape, taps_shape],
        compiler_params=pltpu.CompilerParams(vmem_limit_bytes=16 * 2**20),
    )(result)


def per_device(features, labels, cotangent, first_kernel, holed_kernel, point_weight):
    count = lax.axis_size("dp")
    wide = count >= 32
    dims = {"z_mid": 2 if wide else 1, "z_low": 2 if wide else 1, "x": 4 if wide else 1}
    dims |= {"y_high": count // 32 if wide else 1, "y_low": 2, "z_top": 2, "core": 2}
    total = count * 4
    scale = 1.0 / math.sqrt(total * CELLS)
    slab = lax.axis_index("slab")
    where = slab[None].astype(jnp.int32)
    feats = features[0]
    message, weighted = prepare(
        where, feats, labels.reshape(ROWS, 1, COLS), cotangent.reshape(CELLS, WIDTH), point_weight
    )
    spot, message = lax.optimization_barrier((slab, message))
    row = lax.dynamic_index_in_dim(feats, (ROWS - 1) * (1 - spot % 2), 0, keepdims=False)
    mirrored = [(d, d - d % 4 + 3 - d % 4) for d in range(total)]
    partner = lax.ppermute(message, AXES, mirrored)
    near = lax.ppermute(row, AXES, [(d, d ^ 1) for d in range(total)])

    first, far = first_work(where, feats, near, first_kernel, holed_kernel, point_weight)
    arrived = lax.ppermute(far, AXES, [pair for pair in mirrored if pair[0] % 4 in (0, 3)])

    given = (where, feats, near, partner, weighted, first, first_kernel, holed_kernel, point_weight)
    theirs, own_part = second_work(1, *given)
    swapped = lax.ppermute(theirs, AXES, [(d, d ^ 1) for d in range(total)])
    mine, own = second_work(0, *given)

    cores = device_groups(dims, "core")
    block = device_groups(dims, "z_low", "x", "y_low")
    z_ring = device_groups(dims, "z_top", "z_mid")
    y_ring = device_groups(dims, "y_high")
    mine, arrived = lax.optimization_barrier((mine, arrived))
    units = (mine.astype(F32) + swapped.astype(F32)).astype(BF16).reshape(-1, 8, LANES)
    units = scattered(units, block).astype(BF16)
    units = jnp.sum(gathered(units, z_ring).astype(F32), axis=0).astype(BF16)
    units = (jnp.sum(gathered(units, y_ring).astype(F32), axis=0) * scale).astype(BF16)
    units = gathered(units, block).reshape(-1, 8, LANES)
    result = gathered(units, cores).reshape(2 * PAYLOAD_ROWS, LANES)

    branch_out = (own_part + own + arrived.astype(F32)).astype(BF16).reshape(1, ROWS, COLS, WIDTH)
    point_grad, first_grad, atrous_grad = finish(result)
    return (branch_out, point_grad, first_grad, atrous_grad)


def solution(mesh):
    in_specs = (
        P("dp", "slab", None, None),
        P("dp", "slab", None),
        P("dp", "slab", None, None),
        P(),
        P(),
        P(),
    )
    out_specs = (P("dp", "slab", None, None), P(), P(), P())
    return jax.shard_map(
        per_device, mesh=mesh, in_specs=in_specs, out_specs=out_specs, check_vma=False
    )
```

```python
import itertools
import math

import jax
import jax.numpy as jnp
from jax import lax
from jax.experimental import pallas as pl
from jax.experimental.pallas import tpu as pltpu
from jax.sharding import PartitionSpec as P

AXES = ("dp", "slab")
STEP = 36
ROWS = 12
COLS = 40
CELLS = ROWS * COLS
EDGE = COLS - STEP
CHANNELS = 2048
WIDTH = 256
BLOCK = 512
PACKED = 256
LANES = 128
GRAD_ROWS = 32
HALF = CHANNELS // 2
PAYLOAD_ROWS = 2 * HALF + HALF // LANES * GRAD_ROWS
F32 = jnp.float32
BF16 = jnp.bfloat16


def device_groups(dims, *names):
    strides, stride = {}, 1
    for name in reversed(dims):
        strides[name] = stride
        stride *= dims[name]

    def places(chosen):
        return [
            sum(i * strides[n] for n, i in zip(chosen, spot))
            for spot in itertools.product(*(range(dims[n]) for n in chosen))
        ]

    inside = places(names)
    return [[base + i for i in inside] for base in places([n for n in dims if n not in names])]


def exchange(parts, groups):
    return lax.all_to_all(parts, AXES, 0, 0, axis_index_groups=groups, tiled=True)


def scattered(units, groups):
    count = len(groups[0])
    parts = exchange(units.reshape(count, units.shape[0] // count, 8, LANES), groups)
    return jnp.sum(parts.astype(F32), axis=0)


def gathered(units, groups):
    count = len(groups[0])
    return exchange(jnp.broadcast_to(units[None], (count, *units.shape)), groups)


def widened(xs, x_ref, near, far, slab):
    core = lax.rem(slab, 2)
    one = jnp.where(core == 1, 1.0, 0.0)
    xs[pl.ds(0, COLS), :] = near * one + far * jnp.where(slab == 2, 1.0, 0.0)
    xs[pl.ds((ROWS + 1) * COLS, COLS), :] = near * (1.0 - one) + far * jnp.where(slab == 1, 1.0, 0.0)

    for r in range(ROWS):
        xs[pl.ds((r + 1) * COLS, COLS), :] = x_ref[r].astype(F32)


def from_left(v):
    sub = lax.broadcasted_iota(jnp.int32, (8, v.shape[1]), 0)
    moved = pltpu.roll(v, 1, 0)
    return jnp.concatenate([jnp.where(sub == 0, 0.0, moved[:8]), moved[8:]], 0)


def from_right(v):
    sub = lax.broadcasted_iota(jnp.int32, (8, v.shape[1]), 0)
    moved = pltpu.roll(v, COLS - 1, 0)
    return jnp.concatenate([moved[: COLS - 8], jnp.where(sub == 7, 0.0, moved[COLS - 8 :])], 0)


def fold(v):
    parts = [v[8 * i : 8 * i + 8] for i in range(COLS // 8)]
    while len(parts) > 1:
        parts = [a + b for a, b in zip(parts[::2], parts[1::2])] + (
            parts[-1:] if len(parts) % 2 else []
        )
    return parts[0]


def conv_row(fk, x):
    side = [fk[0][j] * x[0] + fk[1][j] * x[1] + fk[2][j] * x[2] for j in range(3)]
    return side[1] + from_left(side[0]) + from_right(side[2])


def ends(v):
    low = lax.broadcasted_iota(jnp.int32, (8, LANES), 0) < EDGE
    high_end = jnp.where(low, pltpu.roll(v[COLS - 8 :], 4, 0), 0.0)
    low_end = jnp.where(low, 0.0, pltpu.roll(v[:8], 4, 0))
    return high_end, low_end


def spread(k, v, v_ends):
    c = k[1] * v
    return jnp.concatenate(
        [c[:8] + k[2] * v_ends[0], c[8 : COLS - 8], c[COLS - 8 :] + k[0] * v_ends[1]], 0
    )


def taps(ref, lanes):
    return [[ref[i, j : j + 1, lanes] for j in range(3)] for i in range(3)]


def far_taps(hk, slab):
    up = jnp.where(slab == 0, 1.0, 0.0)
    down = jnp.where(slab == 3, 1.0, 0.0)
    return [hk[0][j] * up + hk[2][j] * down for j in range(3)]


def first_body(
    slab_ref, x_ref, near_ref, first_k_ref, holed_k_ref, point_ref, f_ref, far_out_ref, xs, a_far, far_acc
):
    step = pl.program_id(0)
    slab = slab_ref[0]

    @pl.when(step == 0)
    def _():
        far_acc[...] = jnp.zeros_like(far_acc)

    widened(xs, x_ref, near_ref[...].astype(F32), jnp.zeros((COLS, BLOCK), F32), slab)
    for chunk in range(BLOCK // LANES):
        lanes = pl.ds(chunk * LANES, LANES)
        fk = taps(first_k_ref, lanes)
        kf = far_taps(taps(holed_k_ref, lanes), slab)

        for p in range(ROWS // 2):
            base = p * 2 * COLS
            x = [xs[pl.ds(base + i * COLS, COLS), lanes] for i in range(4)]
            far_rows = []
            for r in range(2):
                f16 = conv_row(fk, x[r : r + 3]).astype(BF16)
                f_ref[2 * p + r, :, lanes] = f16
                f = f16.astype(F32)
                far_rows.append(spread(kf, f, ends(f)))
            a_far[pl.ds(base, 2 * COLS), lanes] = jnp.concatenate(far_rows, 0).astype(BF16)

    far_acc[...] += jnp.dot(a_far[...], point_ref[...], preferred_element_type=F32)

    @pl.when(step == pl.num_programs(0) - 1)
    def _():
        far_out_ref[...] = far_acc[...].astype(BF16)


def second_body(
    slab_ref,
    x_ref,
    near_ref,
    far_ref,
    weighted_ref,
    partner_ref,
    f_ref,
    first_k_ref,
    holed_k_ref,
    point_ref,
    payload_ref,
    own_out_ref,
    xs,
    wfar,
    b_own,
    b_far,
    a_own,
    a_far,
    f_edge,
    own_acc,
):
    step = pl.program_id(0)
    slab = slab_ref[0]
    edge = jnp.where(lax.rem(slab, 2) == 0, 0, ROWS - 1)
    up = jnp.where(slab == 0, 1.0, 0.0)
    down = jnp.where(slab == 3, 1.0, 0.0)

    @pl.when(step == 0)
    def _():
        wfar[...] = (partner_ref[...].astype(F32) * (up + down)).astype(BF16)
        own_acc[...] = jnp.zeros_like(own_acc)

    far = far_ref[...].astype(F32)
    far = jnp.concatenate([far[i * COLS : (i + 1) * COLS] for i in range(BLOCK // PACKED)], 1)
    widened(xs, x_ref, near_ref[...].astype(F32), far, slab)

    weights = point_ref[...]
    nt = (((1,), (1,)), ((), ()))
    tn = (((0,), (0,)), ((), ()))
    for given, back in ((weighted_ref, b_own), (wfar, b_far)):
        product = lax.dot_general(given[...], weights, nt, preferred_element_type=F32)
        back[...] = product.astype(BF16).astype(F32)

    for chunk in range(BLOCK // LANES):
        lanes = pl.ds(chunk * LANES, LANES)
        fk = taps(first_k_ref, lanes)
        hk = taps(holed_k_ref, lanes)
        mk = hk[1]
        kf = far_taps(hk, slab)
        x = [xs[pl.ds(pl.multiple_of((edge + i) * COLS, 8), COLS), lanes] for i in range(3)]
        f_edge[...] = conv_row(fk, x).astype(BF16).astype(F32)

        zero = jnp.zeros((8, LANES), F32)
        is_low = lax.broadcasted_iota(jnp.int32, (8, LANES), 0) < EDGE
        first_acc, own_g, far_g = [zero] * 9, [zero] * 3, [zero] * 3
        for p in range(ROWS // 2):
            base = p * 2 * COLS
            own_rows, far_rows = [], []
            for r in range(2):
                here = pl.ds(base + r * COLS, COLS)
                f = f_ref[2 * p + r, :, lanes].astype(F32)
                if 2 * p + r in (0, ROWS - 1):
                    f = jnp.where(2 * p + r == edge, f_edge[...], f)
                bo, bf = b_own[here, lanes], b_far[here, lanes]
                f_ends = ends(f)
                own_rows.append(spread(mk, f, f_ends))
                far_rows.append(spread(kf, f, f_ends))
                for sums, b in ((own_g, bo), (far_g, bf)):
                    sums[0] += f_ends[1] * b[COLS - 8 :]
                    sums[1] += fold(f * b)
                    sums[2] += f_ends[0] * b[:8]
                g = mk[1] * bo + kf[1] * bf
                high = mk[0] * bo[COLS - 8 :] + kf[0] * bf[COLS - 8 :]
                low = mk[2] * bo[:8] + kf[2] * bf[:8]
                high = jnp.where(is_low, pltpu.roll(high, 4, 0), 0.0)
                low = jnp.where(is_low, 0.0, pltpu.roll(low, 4, 0))
                g = jnp.concatenate([g[:8] + high, g[8 : COLS - 8], g[COLS - 8 :] + low], 0)
                g = g.astype(BF16).astype(F32)
                shifted = [from_right(g), g, from_left(g)]
                for i in range(3):
                    x = xs[pl.ds(base + (r + i) * COLS, COLS), lanes]
                    for j in range(3):
                        first_acc[3 * i + j] += fold(x * shifted[j])
            there = pl.ds(base, 2 * COLS)
            a_own[there, lanes] = jnp.concatenate(own_rows, 0).astype(BF16)
            a_far[there, lanes] = jnp.concatenate(far_rows, 0).astype(BF16)

        def line(v):
            return jnp.sum(v, axis=0, keepdims=True)

        far_lines = [line(v) for v in far_g]
        lines = [line(v) for v in first_acc]
        lines += [v * up for v in far_lines]
        lines += [line(v) for v in own_g]
        lines += [v * down for v in far_lines]
        lines.append(jnp.zeros((GRAD_ROWS - len(lines), LANES), F32))
        at = 2 * HALF + (step * (BLOCK // LANES) + chunk) * GRAD_ROWS
        payload_ref[pl.ds(pl.multiple_of(at, GRAD_ROWS), GRAD_ROWS), :] = jnp.concatenate(
            lines, 0
        ).astype(BF16)

    own_acc[...] += jnp.dot(a_own[...], weights, preferred_element_type=F32)
    part = lax.dot_general(a_own[...], weighted_ref[...], tn, preferred_element_type=F32)
    part += lax.dot_general(a_far[...], wfar[...], tn, preferred_element_type=F32)
    for half in range(WIDTH // LANES):
        at = pl.multiple_of(half * HALF + step * BLOCK, BLOCK)
        payload_ref[pl.ds(at, BLOCK), :] = part[:, half * LANES : (half + 1) * LANES].astype(BF16)

    @pl.when(step == pl.num_programs(0) - 1)
    def _():
        own_out_ref[...] = own_acc[...]


def whole(shape):
    return pl.BlockSpec(shape, lambda k, s: (0,) * len(shape))


def kernel_call(body, steps, in_specs, out_specs, out_shape, scratch_shapes, flops):
    return pl.pallas_call(
        body,
        grid_spec=pltpu.PrefetchScalarGridSpec(
            num_scalar_prefetch=1,
            grid=(steps,),
            in_specs=in_specs,
            out_specs=out_specs,
            scratch_shapes=scratch_shapes,
        ),
        out_shape=out_shape,
        compiler_params=pltpu.CompilerParams(vmem_limit_bytes=40 * 2**20),
        cost_estimate=pl.CostEstimate(flops=flops, bytes_accessed=8 * 2**20, transcendentals=0),
    )


def channel_specs(at):
    return (
        pl.BlockSpec((ROWS, COLS, BLOCK), lambda k, s: (0, 0, at(k, s))),
        pl.BlockSpec((COLS, BLOCK), lambda k, s: (0, at(k, s))),
        pl.BlockSpec((3, 3, BLOCK), lambda k, s: (0, 0, at(k, s))),
        pl.BlockSpec((BLOCK, WIDTH), lambda k, s: (at(k, s), 0)),
    )


CELLS_SPEC = whole((CELLS, WIDTH))


def first_work(slab, features, near, first_kernel, holed_kernel, point_weight):
    slab_spec, line_spec, taps_spec, point_spec = channel_specs(lambda k, s: k)
    return kernel_call(
        first_body,
        CHANNELS // BLOCK,
        [slab_spec, line_spec, taps_spec, taps_spec, point_spec],
        [slab_spec, CELLS_SPEC],
        [
            jax.ShapeDtypeStruct((ROWS, COLS, CHANNELS), BF16),
            jax.ShapeDtypeStruct((CELLS, WIDTH), BF16),
        ],
        [
            pltpu.VMEM(((ROWS + 2) * COLS, BLOCK), F32),
            pltpu.VMEM((CELLS, BLOCK), BF16),
            pltpu.VMEM((CELLS, WIDTH), F32),
        ],
        2 * 2 * CELLS * CHANNELS * WIDTH,
    )(slab, features, near, first_kernel, holed_kernel, point_weight)


def second_work(
    other, slab, features, near, partner, weighted, first, first_kernel, holed_kernel, point_weight
):
    packs = BLOCK // PACKED
    steps = HALF // BLOCK
    at = lambda k, s: k + steps * lax.rem(s[0] + other, 2)
    slab_spec, line_spec, taps_spec, point_spec = channel_specs(at)
    return kernel_call(
        second_body,
        steps,
        [
            slab_spec,
            line_spec,
            pl.BlockSpec((packs * COLS, PACKED), lambda k, s: (at(k, s), 0)),
            CELLS_SPEC,
            CELLS_SPEC,
            slab_spec,
            taps_spec,
            taps_spec,
            point_spec,
        ],
        [whole((PAYLOAD_ROWS, LANES)), CELLS_SPEC],
        [
            jax.ShapeDtypeStruct((PAYLOAD_ROWS, LANES), BF16),
            jax.ShapeDtypeStruct((CELLS, WIDTH), F32),
        ],
        [
            pltpu.VMEM(((ROWS + 2) * COLS, BLOCK), F32),
            pltpu.VMEM((CELLS, WIDTH), BF16),
            pltpu.VMEM((CELLS, BLOCK), F32),
            pltpu.VMEM((CELLS, BLOCK), F32),
            pltpu.VMEM((CELLS, BLOCK), BF16),
            pltpu.VMEM((CELLS, BLOCK), BF16),
            pltpu.VMEM((COLS, LANES), F32),
            pltpu.VMEM((CELLS, WIDTH), F32),
        ],
        1000 * 2 * CELLS * HALF * WIDTH,
    )(
        slab,
        features,
        near,
        partner,
        weighted,
        partner,
        first,
        first_kernel,
        holed_kernel,
        point_weight,
    )


def prepare_body(slab_ref, label_ref, cot_ref, far_ref, _, message_ref, weighted_ref):
    slab = slab_ref[0]
    outer = jnp.logical_or(slab == 0, slab == 3)
    diagonal = lax.broadcasted_iota(jnp.int32, (COLS, COLS), 0) == lax.broadcasted_iota(
        jnp.int32, (COLS, COLS), 1
    )
    for p in range(ROWS // 2):
        pair = pl.ds(2 * COLS * p, 2 * COLS)
        columns = []
        for r in range(2 * p, 2 * p + 2):
            label = label_ref[r]
            weight = jnp.where(label == 0, 0.6, jnp.where(label == 1, 2.4, 1.5)).astype(F32)
            spot = jnp.where(diagonal, jnp.broadcast_to(weight, (COLS, COLS)), 0.0)
            columns.append(jnp.sum(spot, axis=1, keepdims=True))
        scaled = (cot_ref[pair, :].astype(F32) * jnp.concatenate(columns, 0)).astype(BF16)
        weighted_ref[pair, :] = scaled

    @pl.when(outer)
    def _():
        message_ref[...] = weighted_ref[...]

    @pl.when(jnp.logical_not(outer))
    def _():
        packs = CHANNELS // PACKED
        for q in range(0, packs, 2):
            two = [far_ref[0, :, (q + i) * PACKED : (q + i + 1) * PACKED].astype(F32) for i in range(2)]
            message_ref[pl.ds(q * COLS, 2 * COLS), :] = jnp.concatenate(two, 0).astype(BF16)
        rest = CELLS - packs * COLS
        message_ref[pl.ds(packs * COLS, rest), :] = jnp.zeros((rest, WIDTH), BF16)


def prepare(slab, features, labels, cotangent, weights):
    far_row = pl.BlockSpec((1, COLS, CHANNELS), lambda k, s: ((ROWS - 1) * lax.rem(s[0], 2), 0, 0))
    cells = jax.ShapeDtypeStruct((CELLS, WIDTH), BF16)
    return pl.pallas_call(
        prepare_body,
        grid_spec=pltpu.PrefetchScalarGridSpec(
            num_scalar_prefetch=1,
            grid=(1,),
            in_specs=[whole((ROWS, 1, COLS)), CELLS_SPEC, far_row, whole((16, WIDTH))],
            out_specs=[CELLS_SPEC, CELLS_SPEC],
        ),
        out_shape=[cells, cells],
        compiler_params=pltpu.CompilerParams(vmem_limit_bytes=56 * 2**20),
    )(slab, labels, cotangent, features, weights)


def finish_body(half_ref, point_ref, first_ref, atrous_ref):
    point_ref[:, :LANES] = half_ref[:HALF, :]
    point_ref[:, LANES:] = half_ref[HALF : 2 * HALF, :]
    for q in range(HALF // LANES):
        lanes = pl.ds(pl.multiple_of(pl.program_id(0) * HALF + q * LANES, LANES), LANES)
        lines = half_ref[2 * HALF + q * GRAD_ROWS : 2 * HALF + (q + 1) * GRAD_ROWS, :].astype(F32)
        for i in range(3):
            first_ref[i, :, lanes] = lines[3 * i : 3 * i + 3]
            atrous_ref[i, :, lanes] = lines[9 + 3 * i : 12 + 3 * i]


def finish(result):
    taps_shape = jax.ShapeDtypeStruct((3, 3, CHANNELS), F32)
    taps_spec = pl.BlockSpec((3, 3, CHANNELS), lambda k: (0, 0, 0))
    return pl.pallas_call(
        finish_body,
        grid=(2,),
        in_specs=[pl.BlockSpec((PAYLOAD_ROWS, LANES), lambda k: (k, 0))],
        out_specs=[pl.BlockSpec((HALF, WIDTH), lambda k: (k, 0)), taps_spec, taps_spec],
        out_shape=[jax.ShapeDtypeStruct((CHANNELS, WIDTH), BF16), taps_shape, taps_shape],
        compiler_params=pltpu.CompilerParams(vmem_limit_bytes=16 * 2**20),
    )(result)


def per_device(features, labels, cotangent, first_kernel, holed_kernel, point_weight):
    count = lax.axis_size("dp")
    wide = count >= 32
    dims = {"z_mid": 2 if wide else 1, "z_low": 2 if wide else 1, "x": 4 if wide else 1}
    dims |= {"y_high": count // 32 if wide else 1, "y_low": 2, "z_top": 2, "core": 2}
    total = count * 4
    scale = 1.0 / math.sqrt(total * CELLS)
    slab = lax.axis_index("slab")
    where = slab[None].astype(jnp.int32)
    feats = features[0]
    message, weighted = prepare(
        where, feats, labels.reshape(ROWS, 1, COLS), cotangent.reshape(CELLS, WIDTH), point_weight
    )
    spot, message = lax.optimization_barrier((slab, message))
    row = lax.dynamic_index_in_dim(feats, (ROWS - 1) * (1 - spot % 2), 0, keepdims=False)
    mirrored = [(d, d - d % 4 + 3 - d % 4) for d in range(total)]
    partner = lax.ppermute(message, AXES, mirrored)
    near = lax.ppermute(row, AXES, [(d, d ^ 1) for d in range(total)])

    first, far = first_work(where, feats, near, first_kernel, holed_kernel, point_weight)
    arrived = lax.ppermute(far, AXES, [pair for pair in mirrored if pair[0] % 4 in (0, 3)])

    given = (where, feats, near, partner, weighted, first, first_kernel, holed_kernel, point_weight)
    theirs, own_part = second_work(1, *given)
    swapped = lax.ppermute(theirs, AXES, [(d, d ^ 1) for d in range(total)])
    mine, own = second_work(0, *given)

    cores = device_groups(dims, "core")
    block = device_groups(dims, "z_low", "x", "y_low")
    z_ring = device_groups(dims, "z_top", "z_mid")
    y_ring = device_groups(dims, "y_high")
    mine, arrived = lax.optimization_barrier((mine, arrived))
    units = (mine.astype(F32) + swapped.astype(F32)).astype(BF16).reshape(-1, 8, LANES)
    units = scattered(units, block).astype(BF16)
    units = jnp.sum(gathered(units, z_ring).astype(F32), axis=0).astype(BF16)
    units = (jnp.sum(gathered(units, y_ring).astype(F32), axis=0) * scale).astype(BF16)
    units = gathered(units, block).reshape(-1, 8, LANES)
    result = gathered(units, cores).reshape(2 * PAYLOAD_ROWS, LANES)

    branch_out = (own_part + own + arrived.astype(F32)).astype(BF16).reshape(1, ROWS, COLS, WIDTH)
    point_grad, first_grad, atrous_grad = finish(result)
    return (branch_out, point_grad, first_grad, atrous_grad)


def solution(mesh):
    in_specs = (
        P("dp", "slab", None, None),
        P("dp", "slab", None),
        P("dp", "slab", None, None),
        P(),
        P(),
        P(),
    )
    out_specs = (P("dp", "slab", None, None), P(), P(), P())
    return jax.shard_map(
        per_device, mesh=mesh, in_specs=in_specs, out_specs=out_specs, check_vma=False
    )
```
